512 devices in a mesh: tiles: 128 (over y, z, core), grp: 4 (over x).
Axes of the slice: x: 4, y: 4, z: 16, core: 2. Of those that a mesh axis runs over, the one named last changes fastest.
Arguments:
- features: bfloat16 [4, 384, 8, 8, 512], P('grp', 'tiles'), may hold values from -6 to 6
- occupancy: int32 [4, 384, 8, 64], P('grp', 'tiles'), may hold values from 0 to 1, as said below
- neighbour_owner: int32 [4, 384, 8], P('grp', 'tiles'), may hold values from -1 to 127, as said below
- neighbour_slot: int32 [4, 384, 8], P('grp', 'tiles'), may hold values from -1 to 2, as said below
- parent_map: int32 [4, 384, 2], P('grp', 'tiles'), may hold values from -1 to 127, as said below
- parent_children: int32 [4, 128, 4, 2], P('grp', 'tiles'), may hold values from -1 to 127, as said below
- conv_weight: bfloat16 [1728, 64], replicated, may hold values from -0.15625 to 0.15625
- down_weight: bfloat16 [512, 128], replicated, may hold values from -0.25 to 0.25
- parent_cot: bfloat16 [4, 128, 8, 8, 512], P('grp', 'tiles'), may hold values from -6 to 6
Outputs:
- parent_out: bfloat16 [4, 128, 8, 8, 512], P('grp', 'tiles')
- grad_conv: float32 [1728, 64], replicated
- grad_down: float32 [512, 128], replicated
The draws below stay inside these ranges and needn't reach their ends.
Inputs may be any that keep to these rules, and one draw needn't show every extreme that they name: `occupancy`: 0 or 1; slots that hold no tile are all zeros. `neighbour_owner`: -1 where there is no neighbour. An owner lies within two indices of the tile's own device; a neighbour on a higher index never has dx = -1, one on a lower index never has dx = 1. Neighbourhood is symmetric: if A names B in direction k, B names A in direction 7 - k. `neighbour_slot`: -1 exactly where the owner is -1. `parent_map`: column 0: the parent's owner, the tile's own device or one or two indices lower, -1 for an empty slot; column 1: the quadrant 0 to 3 (-1 for an empty slot). Each parent quadrant is named by at most one tile, and parent_children names the same pairs. `parent_children`: owner and slot of the child in each quadrant, or -1 in both; child owners are the parent's device or up to two indices higher.
All inputs are finite; a program needn't handle non-finite values.
Results may differ from the reference program's by a relative error of at most 0.0049.
Values may be sent and summed in bfloat16 or wider, within the bound.
No kernel may reach another device: no remote copies, remote signals or barrier semaphores. Data moves between devices by JAX's collectives and lax.ppermute only.
A program may use at most 128 MiB of HBM per device.

```python
import math
import jax
import jax.numpy as jnp
from jax import lax

TILE = 8
CH = 64
PCH = 128
TPD = 3
SLOTS = 384
PARENTS = 128
N_TILES = 128
N_GRP = 4


STEP_X = (-1, -1, -1, 0, 0, 1, 1, 1)


STEP_Y = (-1, 0, 1, -1, 1, -1, 0, 1)


def layout(key):
    extra = jax.random.randint(key, (N_GRP, N_TILES), 0, 2)
    counts = 2 + extra
    counts = counts.at[:, 0].set(3).at[:, 1].set(2).at[:, 2].set(2)
    starts = jnp.cumsum(counts, axis=1) - counts
    totals = jnp.sum(counts, axis=1)
    return (counts, starts, totals)


def owner_of(ranks, starts):
    shape = ranks.shape
    flat = ranks.reshape(N_GRP, -1)
    owner = jnp.sum((starts[:, None, :] <= flat[:, :, None]).astype(jnp.int32), axis=-1) - 1
    owner = jnp.maximum(owner, 0)
    slot = flat - jnp.take_along_axis(starts, owner, axis=1)
    return (owner.reshape(shape), slot.reshape(shape))


def geometry(key):
    counts, starts, totals = layout(key)
    slots = N_TILES * TPD
    device = jnp.arange(slots, dtype=jnp.int32) // TPD
    within = jnp.arange(slots, dtype=jnp.int32) % TPD
    rank = starts[:, device] + within[None, :]
    used = within[None, :] < counts[:, device]
    xpos = rank // 2
    ypos = rank % 2
    next_x = xpos[..., None] + jnp.array(STEP_X, jnp.int32)
    next_y = ypos[..., None] + jnp.array(STEP_Y, jnp.int32)
    next_rank = 2 * next_x + next_y
    valid = used[..., None] & (next_y >= 0) & (next_y <= 1) & (next_x >= 0) & (next_rank < totals[:, None, None])
    owner, slot = owner_of(jnp.where(valid, next_rank, 0), starts)
    nb_owner = jnp.where(valid, owner, -1)
    nb_slot = jnp.where(valid, slot, -1)
    powner, pslot = owner_of(rank // 4 * 4, starts)
    pmap = jnp.stack([jnp.where(used, powner, -1), jnp.where(used, rank % 4, -1)], axis=-1)
    first = (starts + 3) // 4 * 4
    owns = (first < starts + counts) & (first < totals[:, None])
    child_rank = first[..., None] + jnp.arange(4, dtype=jnp.int32)
    child_ok = owns[..., None] & (child_rank < totals[:, None, None])
    cowner, cslot = owner_of(jnp.where(child_ok, child_rank, 0), starts)
    pchild = jnp.stack([jnp.where(child_ok, cowner, -1), jnp.where(child_ok, cslot, -1)], axis=-1)
    return (nb_owner.astype(jnp.int32), nb_slot.astype(jnp.int32), pmap.astype(jnp.int32), pchild.astype(jnp.int32))


def draw_neighbour_owner(key, part):
    return geometry(key)[0]


def draw_neighbour_slot(key, part):
    return geometry(key)[1]


def draw_parent_map(key, part):
    return geometry(key)[2]


def draw_parent_children(key, part):
    return geometry(key)[3]


def draw_occupancy(key, part):
    counts, starts, totals = layout(key)
    key = jax.random.fold_in(key, 11)
    key_flip, key_thick, key_base, key_fill = jax.random.split(key, 4)
    slots = N_TILES * TPD
    device = jnp.arange(slots, dtype=jnp.int32) // TPD
    within = jnp.arange(slots, dtype=jnp.int32) % TPD
    used = within[None, :] < counts[:, device]
    flip = jax.random.randint(key_flip, (N_GRP, 1), 0, 2)
    place = jnp.where(flip == 1, N_TILES - 1 - device[None, :], device[None, :])
    thick = TILE // 4 + place * (TILE // 2) // N_TILES + jax.random.randint(key_thick, (N_GRP, slots), 0, TILE // 4 + 1)
    base = jax.random.randint(key_base, (N_GRP, slots, TILE, TILE), 0, TILE - thick[:, :, None, None] + 1)
    depth = jnp.arange(TILE, dtype=jnp.int32)
    band = (depth >= base[..., None]) & (depth < base[..., None] + thick[:, :, None, None, None])
    fill = jax.random.randint(key_fill, (N_GRP, slots, TILE, TILE, TILE), 0, 8) < 6
    occupied = band & fill & used[:, :, None, None, None]
    return occupied.astype(jnp.int32).reshape(N_GRP, slots, TILE, TILE * TILE)


def block_levels(own_key, dims, cuts, low, top_value):
    def one(position, shards_of):
        draws = jax.random.uniform(jax.random.fold_in(jax.random.fold_in(own_key, 6), position), (shards_of,), jnp.float32, low / len(cuts), top_value / len(cuts))
        return jnp.repeat(jnp.exp(draws), dims[position] // shards_of).reshape((-1,) + (1,) * (len(dims) - position - 1))

    gain = one(*cuts[0])
    for cut in cuts[1:]:
        gain = gain * one(*cut)
    return gain


def noise(own_key, dims, scale, limit, cuts=(), kind=jnp.bfloat16):
    level = block_levels(own_key, dims, cuts, -0.22, 0.18) if cuts else 1.0
    values = jax.random.normal(own_key, dims, jnp.float32) * scale * level
    return jnp.minimum(jnp.maximum(values, -limit), limit).astype(kind)


def setup_inputs(seed: int = 0) -> dict:
    arg_keys = jax.random.split(jax.random.key(seed), 10)
    features = noise(arg_keys[0], (N_GRP, SLOTS, TILE, TILE, TILE * CH), 1.0, 6.0, ((0, 4), (1, 128)))
    occupancy = draw_occupancy(jax.random.fold_in(arg_keys[9], 71), 0)
    neighbour_owner = draw_neighbour_owner(jax.random.fold_in(arg_keys[9], 71), 0)
    neighbour_slot = draw_neighbour_slot(jax.random.fold_in(arg_keys[9], 71), 0)
    parent_map = draw_parent_map(jax.random.fold_in(arg_keys[9], 71), 0)
    parent_children = draw_parent_children(jax.random.fold_in(arg_keys[9], 71), 0)
    conv_weight = noise(arg_keys[6], (27 * CH, CH), (27 * CH) ** -0.5, 0.15625)
    down_weight = noise(arg_keys[7], (8 * CH, PCH), (8 * CH) ** -0.5, 0.25)
    parent_cot = noise(arg_keys[8], (N_GRP, PARENTS, TILE, TILE, TILE * PCH // 2), 1.0, 6.0, ((0, 4), (1, 128)))
    return {"features": features, "occupancy": occupancy, "neighbour_owner": neighbour_owner, "neighbour_slot": neighbour_slot, "parent_map": parent_map, "parent_children": parent_children, "conv_weight": conv_weight, "down_weight": down_weight, "parent_cot": parent_cot}


FACE_DIR = (1, 6, 3, 4)
FACE_TAKE = (1, 0, 3, 2)
CORNER_DIR = (0, 2, 5, 7)
CORNER_TAKE = (3, 2, 1, 0)

def tile_rims(tiles, edge):
    count = tiles.shape[0]
    width = tiles.shape[3]
    faces = jnp.stack([tiles[:, 0], tiles[:, edge - 1], tiles[:, :, 0], tiles[:, :, edge - 1]], axis=1)
    corners = jnp.stack([tiles[:, 0, 0], tiles[:, 0, edge - 1], tiles[:, edge - 1, 0], tiles[:, edge - 1, edge - 1]], axis=1)
    return jnp.concatenate([faces.reshape(count, 4 * edge, width), corners], axis=1)

def padded(tiles, sides, corners, chans):
    middle = jnp.concatenate([sides[:, 2][:, :, None], tiles, sides[:, 3][:, :, None]], axis=2)
    first = jnp.concatenate([corners[:, 0:1], sides[:, 0], corners[:, 1:2]], axis=1)
    last = jnp.concatenate([corners[:, 2:3], sides[:, 1], corners[:, 3:4]], axis=1)
    full = jnp.concatenate([first[:, None], middle, last[:, None]], axis=1)
    return jnp.pad(full, ((0, 0), (0, 0), (0, 0), (chans, chans)))

def windows(full, row_off, col_off, chans):
    count = full.shape[0]
    edge = full.shape[1] - 2
    part = full[:, row_off:row_off + edge, col_off:col_off + edge].reshape(count, edge, edge, edge + 2, chans)
    stacked = jnp.concatenate([part[:, :, :, depth:depth + edge] for depth in range(3)], axis=-1)
    return stacked.reshape(count * edge ** 3, 3 * chans)

def convolve(full, weight, chans):
    total = None
    for row_off in range(3):
        for col_off in range(3):
            first_row = (3 * row_off + col_off) * 3 * chans
            term = jnp.dot(windows(full, row_off, col_off, chans), weight[first_row:first_row + 3 * chans], preferred_element_type=jnp.float32)
            total = term if total is None else total + term
    return total

def blocks(values, count, edge, chans):
    half = edge // 2
    shaped = values.reshape(count, half, 2, half, 2, half, 2, chans).transpose(0, 1, 3, 5, 2, 4, 6, 7)
    return shaped.reshape(count * half ** 3, 8 * chans)

def unblock(values, count, edge, chans):
    half = edge // 2
    shaped = values.reshape(count, half, half, half, 2, 2, 2, chans).transpose(0, 1, 4, 2, 5, 3, 6, 7)
    return shaped.reshape(count * edge ** 3, chans)

def forward_part(full, occupied, conv_weight, down_weight):
    count = full.shape[0]
    edge = full.shape[1] - 2
    half = edge // 2
    chans = conv_weight.shape[1]
    preact = convolve(full, conv_weight, chans)
    hidden = (jax.nn.silu(preact) * occupied).astype(jnp.bfloat16)
    coarse = occupied.reshape(count, half, 2, half, 2, half, 2).max(axis=(2, 4, 6)).reshape(-1, 1)
    stacked = blocks(hidden, count, edge, chans)
    quads = (jnp.dot(stacked, down_weight, preferred_element_type=jnp.float32) * coarse).astype(jnp.bfloat16)
    return (preact, stacked, coarse, quads)

def backward_down(cot_quads, coarse, stacked, down_weight, count, edge, chans):
    masked = cot_quads * coarse.astype(jnp.bfloat16)
    grad_down = jnp.dot(stacked.T, masked, preferred_element_type=jnp.float32)
    back = unblock(jnp.dot(masked, down_weight.T, preferred_element_type=jnp.float32), count, edge, chans)
    return (grad_down, back)

def backward_conv(full, preact, back, occupied, chans):
    sigma = jax.nn.sigmoid(preact)
    delta = (back * sigma * (1.0 + preact * (1.0 - sigma)) * occupied).astype(jnp.bfloat16)
    pieces = []
    for row_off in range(3):
        for col_off in range(3):
            pieces.append(jnp.dot(windows(full, row_off, col_off, chans).T, delta, preferred_element_type=jnp.float32))
    return jnp.concatenate(pieces, axis=0)

def reference(features, occupancy, neighbour_owner, neighbour_slot, parent_map, parent_children, conv_weight, down_weight, parent_cot):
    edge = TILE
    half = edge // 2
    width = edge * CH
    slots = N_TILES * TPD
    scale = 1.0 / math.sqrt(N_GRP * slots * edge ** 3)
    outputs = []
    conv_total = jnp.zeros((27 * CH, CH), jnp.float32)
    down_total = jnp.zeros((8 * CH, PCH), jnp.float32)
    for region in range(N_GRP):
        occ = occupancy[region].reshape(slots, edge, edge, edge).astype(jnp.float32)
        spread = jnp.broadcast_to(occ[..., None], (slots, edge, edge, edge, CH)).reshape(slots, edge, edge, width)
        tiles = features[region] * spread.astype(jnp.bfloat16)
        rims = tile_rims(tiles, edge)
        faces = rims[:, :4 * edge].reshape(slots, 4, edge, width)
        corners = rims[:, 4 * edge:]
        owner = neighbour_owner[region]
        present = owner >= 0
        source = jnp.where(present, owner * TPD + neighbour_slot[region], 0).astype(jnp.int32)
        sides = jnp.stack([faces[source[:, FACE_DIR[j]], FACE_TAKE[j]] * present[:, FACE_DIR[j], None, None].astype(jnp.bfloat16) for j in range(4)], axis=1)
        corner_in = jnp.stack([corners[source[:, CORNER_DIR[j]], CORNER_TAKE[j]] * present[:, CORNER_DIR[j], None].astype(jnp.bfloat16) for j in range(4)], axis=1)
        quarters = parent_cot[region].reshape(N_TILES, 2, half, 2, half, half * PCH).transpose(0, 1, 3, 2, 4, 5)
        quarters = quarters.reshape(N_TILES, 4, half ** 3, PCH)
        powner = jnp.maximum(parent_map[region][:, 0], 0)
        pquad = jnp.maximum(parent_map[region][:, 1], 0)
        cot_child = quarters[powner, pquad]
        occ_rows = occ.reshape(slots, edge ** 3, 1)

        def tile_step(carry, item):
            tile, side, corner, occupied, cot_quads = item
            full = padded(tile[None], side[None], corner[None], CH)
            preact, stacked, coarse, quads = forward_part(full, occupied, conv_weight, down_weight)
            grad_down, back = backward_down(cot_quads, coarse, stacked, down_weight, 1, edge, CH)
            grad_conv = backward_conv(full, preact, back, occupied, CH)
            return ((carry[0] + grad_conv, carry[1] + grad_down), quads)
        zeros = (jnp.zeros((27 * CH, CH), jnp.float32), jnp.zeros((8 * CH, PCH), jnp.float32))
        sums, quads_all = lax.scan(tile_step, zeros, (tiles, sides, corner_in, occ_rows, cot_child))
        conv_total = conv_total + sums[0]
        down_total = down_total + sums[1]
        kids = parent_children[region]
        kid_ok = kids[..., 0] >= 0
        kid_source = jnp.where(kid_ok, kids[..., 0] * TPD + kids[..., 1], 0).astype(jnp.int32)
        gathered = quads_all[kid_source] * kid_ok[..., None, None].astype(jnp.bfloat16)
        parent = gathered.reshape(N_TILES, 2, 2, half, half, half * PCH).transpose(0, 1, 3, 2, 4, 5)
        outputs.append(parent.reshape(N_TILES, edge, edge, half * PCH))
    return (jnp.stack(outputs, axis=0), conv_total * scale, down_total * scale)
```

```python
import math

import jax
import jax.numpy as jnp
from jax import lax
from jax.experimental import pallas as pl
from jax.experimental.pallas import tpu as pltpu
from jax.sharding import Mesh
from jax.sharding import PartitionSpec as P

BF = jnp.bfloat16
F32 = jnp.float32
TILES = ("y", "z", "core")
NEAR = ("y", "core", "grp")
FAR = ("z",)
DIRS = ((-1, -1), (-1, 0), (-1, 1), (0, -1), (0, 1), (1, -1), (1, 0), (1, 1))
POOL_BASE = {-1: 192, -2: 272, 1: 352, 2: 432}
DOWN_ROWS = 512
GRAD_ROWS = 1536
VMEM = pl.BlockSpec(memory_space=pltpu.VMEM)
SMEM = pl.BlockSpec(memory_space=pltpu.SMEM)
PARAMS = pltpu.CompilerParams(vmem_limit_bytes=40 * 1024 * 1024)


def iota(shape, dim):
    return lax.broadcasted_iota(jnp.int32, shape, dim)


def one_hot(hits):
    return jnp.where(hits, 1.0, 0.0).astype(BF)


def dot(a, b):
    return jnp.dot(a, b, preferred_element_type=F32)


def permuted_y(row):
    return (row & 3) * 2 + ((row >> 2) & 1)


def occ_wide(occ_ref, order):
    occ = occ_ref[...].astype(F32)
    rows = jnp.broadcast_to(occ[:, None, :], (24, 8, 64)).reshape(192, 64)
    keep = (iota((192, 64), 1) >> 3) == order(iota((192, 64), 0) & 7)
    spread = one_hot((iota((64, 512), 0) & 7) == (iota((64, 512), 1) >> 6))
    return dot(jnp.where(keep, rows, 0.0).astype(BF), spread)


def send_kernel(feat_ref, occ_ref, cot_ref, own_ref, up_ref, down_ref):
    occ = occ_wide(occ_ref, lambda y: y)
    own = (feat_ref[...].astype(F32) * occ).astype(BF)
    own_ref[...] = own
    row = iota((80, 192), 0)
    col = iota((80, 192), 1)
    tile = (row >= 24).astype(jnp.int32) + (row >= 48).astype(jnp.int32)
    within = row - tile * 24
    kind = within >> 3
    place = within & 7
    for ref, first, plane in ((up_ref, 64, 7), (down_ref, 0, 0)):
        src = jnp.where(
            kind == 0, plane * 8 + place, jnp.where(kind == 1, place * 8, place * 8 + 7)
        )
        src = jnp.where(row < 72, src + tile * 64, -1)
        ref[first : first + 80, :] = dot(one_hot(src == col), own).astype(BF)
    up_ref[0:64, :] = cot_ref[...]


def prep_kernel(owner_ref, slot_ref, pmap_ref, occ_ref, w_ref, s_ref, sc_ref, bw_ref, occ_out, pocc_out):
    me = lax.axis_index(TILES)
    row = iota((240, 128), 0)
    lane = iota((240, 128), 1)
    off_y = (row >= 80).astype(jnp.int32) + (row >= 160).astype(jnp.int32)
    rest = row - off_y * 80
    px = rest >> 3
    py = permuted_y(rest & 7) + off_y
    sx = (px + 7) & 7
    sy = (py + 7) & 7
    side_x = (px == 9).astype(jnp.int32) - (px == 0).astype(jnp.int32)
    side_y = (py == 9).astype(jnp.int32) - (py == 0).astype(jnp.int32)
    masks = [(side_x == dx) & (side_y == dy) for dx, dy in DIRS]
    own_row = sx * 8 + sy
    for t in range(3):
        index = own_row + t * 64
        for k, (dx, dy) in enumerate(DIRS):
            owner = owner_ref[0, t, k]
            slot = slot_ref[0, t, k]
            off = owner - me
            here = off == 0
            base = jnp.where(
                off == -1,
                POOL_BASE[-1],
                jnp.where(off == -2, POOL_BASE[-2], jnp.where(off == 1, POOL_BASE[1], POOL_BASE[2])),
            )
            if dx:
                face, by_x, by_y = 0, 0, 1
            else:
                face, by_x, by_y = (16 if dy < 0 else 8), 1, 0
            first = jnp.where(here, slot * 64, base + slot * 24 + face)
            by_x = jnp.where(here, 8, by_x)
            by_y = jnp.where(here, 1, by_y)
            source = jnp.where(owner >= 0, first + sx * by_x + sy * by_y, -1)
            index = jnp.where(masks[k], source, index)
        for block in range(4):
            s_ref[t * 240 : (t + 1) * 240, block * 128 : (block + 1) * 128] = one_hot(
                index == lane + block * 128
            )
    row = iota((64, 256), 0)
    lane = iota((64, 256), 1)
    for t in range(3):
        owner = pmap_ref[0, t, 0]
        quad = pmap_ref[0, t, 1]
        first = (me - owner) * 64 + (quad >> 1) * 32 + (quad & 1) * 4
        index = jnp.where(owner >= 0, first + (row >> 4) * 8 + (row & 3), -1)
        sc_ref[t * 64 : (t + 1) * 64, :] = one_hot(index == lane)
    zero = jnp.zeros((64, 64), F32)
    for ab in range(9):
        w0, w1, w2 = (
            w_ref[(3 * ab + d) * 64 : (3 * ab + d + 1) * 64, :].astype(F32) for d in range(3)
        )
        bw_ref[ab * 128 : ab * 128 + 64, :] = jnp.concatenate([w2, w1, w0, zero], axis=1).astype(BF)
        bw_ref[ab * 128 + 64 : ab * 128 + 128, :] = jnp.concatenate(
            [zero, w2, w1, w0], axis=1
        ).astype(BF)
    occ = occ_wide(occ_ref, permuted_y)
    occ_out[...] = occ.astype(BF)
    wide = occ.reshape(12, 2, 8, 512)
    wide = jnp.maximum(wide[:, 0], wide[:, 1]).reshape(96, 512)
    for q in range(4):
        part = wide[:, q * 128 : (q + 1) * 128]
        part = jnp.maximum(part, pltpu.roll(part, 64, 1))
        part = part.reshape(12, 8, 128)
        part = jnp.maximum(part, pltpu.roll(part, 4, 1))
        pocc_out[:, q * 128 : (q + 1) * 128] = part.reshape(96, 128).astype(BF)


def main_kernel(
    own_ref, up1_ref, up2_ref, dn1_ref, dn2_ref, cot_ref, s_ref, sc_ref, bw_ref, occ_ref, pocc_ref,
    down_ref, quad_ref, grad_ref, xc_ref, dt_ref,
):
    pool = jnp.concatenate(
        [own_ref[...], up1_ref[64:144, :], up2_ref[64:144, :], dn1_ref[...], dn2_ref[...]], axis=0
    )
    for t in range(3):
        got = dot(s_ref[t * 240 : (t + 1) * 240, :], pool)
        for b in range(3):
            for a in range(3):
                part = got[b * 80 + a * 8 : b * 80 + a * 8 + 64].astype(BF)
                ab = 3 * a + b
                for m in range(4):
                    xc_ref[m, t * 64 : (t + 1) * 64, ab * 128 : (ab + 1) * 128] = part[
                        :, m * 128 : (m + 1) * 128
                    ]
    taps = bw_ref[...]
    outs = [dot(xc_ref[m], taps) for m in range(4)]
    shifted = []
    for j in range(5):
        total = None
        if j < 4:
            total = outs[j][:, 0:128]
        if j > 0:
            other = outs[j - 1][:, 128:256]
            total = other if total is None else total + other
        shifted.append(pltpu.roll(total, 64, 1))
    low = iota((192, 128), 1) < 64
    left = iota((192, 128), 0) & 7
    first_y = left < 4
    even_x = (iota((192, 128), 0) & 8) == 0
    down = down_ref[...]
    down_cat = jnp.concatenate([down[ij * 128 : (ij + 1) * 128] for ij in range(4)], axis=1)
    cots = jnp.concatenate(
        [cot_ref[...], up1_ref[0:64, :], up2_ref[0:64, :], jnp.zeros((64, 512), BF)], axis=0
    )
    cot = dot(sc_ref[...], cots)
    pocc = pocc_ref[...].astype(F32)
    first_half = (iota((12, 8, 128), 1) & 7) < 4
    grad_down = None
    zeros = jnp.zeros((192, 128), F32)
    dt_ref[0:64, :] = jnp.zeros((64, 192), BF)
    dt_ref[576:640, :] = jnp.zeros((64, 192), BF)
    for q in range(4):
        lanes = slice(q * 128, (q + 1) * 128)
        pre = jnp.where(low, shifted[q], shifted[q + 1])
        occ = occ_ref[:, lanes].astype(F32)
        sigma = 1.0 / (1.0 + jnp.exp(-pre))
        hidden = (pre * sigma * occ).astype(BF)
        prod = dot(hidden, down_cat).reshape(12, 2, 8, 512)
        coarse = jnp.where(first_half, prod[:, 0, :, 0:128], prod[:, 0, :, 128:256]) + jnp.where(
            first_half, prod[:, 1, :, 256:384], prod[:, 1, :, 384:512]
        )
        coarse = coarse + pltpu.roll(coarse, 4, 1)
        pocc_q = pocc[:, lanes].reshape(12, 8, 128)
        coarse = (coarse * pocc_q).reshape(6, 2, 8, 128)
        coarse = jnp.where(first_half[0:6], coarse[:, 0], coarse[:, 1])
        quad_ref[:, lanes] = coarse.reshape(48, 128).astype(BF)
        pocc_rows = jnp.broadcast_to(pocc_q[:, None], (12, 2, 8, 128)).reshape(192, 128)
        gq = cot[:, lanes] * pocc_rows
        gq_bf = gq.astype(BF)
        back = lax.dot_general(gq_bf, down, (((1,), (1,)), ((), ())), preferred_element_type=F32)
        back = jnp.where(
            even_x,
            jnp.where(first_y, back[:, 0:128], back[:, 128:256]),
            jnp.where(first_y, back[:, 256:384], back[:, 384:512]),
        )
        split = jnp.concatenate(
            [
                jnp.where(even_x & first_y, gq, zeros),
                jnp.where(even_x & ~first_y, gq, zeros),
                jnp.where(~even_x & first_y, gq, zeros),
                jnp.where(~even_x & ~first_y, gq, zeros),
            ],
            axis=1,
        ).astype(BF)
        term = lax.dot_general(hidden, split, (((0,), (0,)), ((), ())), preferred_element_type=F32)
        grad_down = term if grad_down is None else grad_down + term
        delta = back * sigma * (1.0 + pre * (1.0 - sigma)) * occ
        dt_ref[64 + q * 128 : 64 + (q + 1) * 128, :] = delta.T.astype(BF)
    for ij in range(4):
        grad_ref[ij * 128 : (ij + 1) * 128, :] = grad_down[:, ij * 128 : (ij + 1) * 128].astype(BF)
    low = iota((64, 128), 1) < 64
    gconv = None
    for m in range(4):
        term = dot(dt_ref[m * 128 : m * 128 + 256, :], xc_ref[m])
        gconv = term if gconv is None else gconv + term
    held = None
    for ab in range(9):
        part = gconv[:, ab * 128 : (ab + 1) * 128]
        rows = [part[e * 64 : (e + 1) * 64] for e in range(4)]
        for d in range(3):
            value = jnp.where(low, rows[2 - d], rows[3 - d])
            value = value + pltpu.roll(value, 64, 1)
            tap = 3 * ab + d
            if tap % 2 == 0 and tap < 26:
                held = value
            else:
                pair = tap // 2
                both = jnp.where(low, held, value) if tap < 26 else jnp.where(low, value, 0.0)
                grad_ref[DOWN_ROWS + pair * 64 : DOWN_ROWS + (pair + 1) * 64, :] = both.astype(BF)
    grad_ref[DOWN_ROWS + 896 :, :] = jnp.zeros((GRAD_ROWS - DOWN_ROWS - 896, 128), BF)


def sum_kernel(parts_ref, out_ref):
    total = jnp.sum(parts_ref[...].astype(F32), axis=0).astype(BF)
    for i in range(out_ref.shape[0]):
        out_ref[i] = total


def final_kernel(scale, kids_ref, quad_ref, q1_ref, q2_ref, grad_ref, parent_ref, conv_ref, down_ref):
    me = lax.axis_index(TILES)
    row = iota((64, 256), 0)
    lane = iota((64, 256), 1)
    which = ((row >> 5) & 1) * 2 + ((row >> 2) & 1)
    index = jnp.full((64, 256), -1, jnp.int32)
    for q in range(4):
        owner = kids_ref[0, 0, q, 0]
        first = (owner - me) * 48 + kids_ref[0, 0, q, 1] * 16
        source = jnp.where(owner >= 0, first + ((row >> 3) & 3) * 4 + (row & 3), -1)
        index = jnp.where(which == q, source, index)
    pool = jnp.concatenate(
        [quad_ref[...], q1_ref[...], q2_ref[...], jnp.zeros((112, 512), BF)], axis=0
    )
    parent_ref[...] = dot(one_hot(index == lane), pool).astype(BF)
    down_ref[...] = grad_ref[0:DOWN_ROWS, :].astype(F32) * scale
    for pair in range(14):
        block = grad_ref[DOWN_ROWS + pair * 64 : DOWN_ROWS + (pair + 1) * 64, :].astype(F32) * scale
        turned = block.T
        if pair < 13:
            conv_ref[pair * 128 : (pair + 1) * 128, :] = turned
        else:
            conv_ref[pair * 128 : pair * 128 + 64, :] = turned[0:64]


def passed_along(shard, by):
    devices = lax.axis_size(TILES)
    pairs = [(i, i + by) for i in range(devices) if 0 <= i + by < devices]
    return lax.ppermute(shard, TILES, pairs)


def exchange(parts, axes):
    return lax.all_to_all(parts, axes, split_axis=0, concat_axis=0, tiled=True)


def body(
    features,
    occupancy,
    neighbour_owner,
    neighbour_slot,
    parent_map,
    parent_children,
    conv_weight,
    down_weight,
    parent_cot,
):
    shape = jax.ShapeDtypeStruct
    scale = 1.0 / math.sqrt(lax.axis_size("grp") * lax.axis_size(TILES) * 3 * 8**3)
    near, far = lax.axis_size(NEAR), lax.axis_size(FAR)
    feats = features.reshape(192, 512)
    occ = occupancy.reshape(24, 64)
    cot = parent_cot.reshape(64, 512)
    own, up, down = pl.pallas_call(
        send_kernel,
        out_shape=(shape((192, 512), BF), shape((144, 512), BF), shape((80, 512), BF)),
        in_specs=[VMEM] * 3,
        out_specs=(VMEM,) * 3,
        compiler_params=PARAMS,
        name="send",
    )(feats, occ, cot)
    up1, up2 = passed_along(up, 1), passed_along(up, 2)
    dn1, dn2 = passed_along(down, -1), passed_along(down, -2)
    pick, pick_cot, taps, occ_rows, pocc_rows = pl.pallas_call(
        prep_kernel,
        out_shape=(
            shape((720, 512), BF),
            shape((192, 256), BF),
            shape((1152, 256), BF),
            shape((192, 512), BF),
            shape((96, 512), BF),
        ),
        in_specs=[SMEM, SMEM, SMEM, VMEM, VMEM],
        out_specs=(VMEM,) * 5,
        compiler_params=PARAMS,
        cost_estimate=pl.CostEstimate(flops=10_000_000, bytes_accessed=4_000_000, transcendentals=0),
        name="prep",
    )(neighbour_owner, neighbour_slot, parent_map, occ, conv_weight)
    quads, grads = pl.pallas_call(
        main_kernel,
        out_shape=(shape((48, 512), BF), shape((GRAD_ROWS, 128), BF)),
        in_specs=[VMEM] * 12,
        out_specs=(VMEM,) * 2,
        scratch_shapes=[pltpu.VMEM((4, 192, 1152), BF), pltpu.VMEM((640, 192), BF)],
        compiler_params=PARAMS,
        name="main",
    )(own, up1, up2, dn1, dn2, cot, pick, pick_cot, taps, occ_rows, pocc_rows, down_weight)
    quads1, quads2 = passed_along(quads, -1), passed_along(quads, -2)
    rows = GRAD_ROWS // near
    parts = exchange(grads.reshape(near, rows, 128), NEAR)

    def summed(parts, copies):
        return pl.pallas_call(
            sum_kernel,
            out_shape=shape((copies, rows, 128), BF),
            in_specs=[VMEM],
            out_specs=VMEM,
            compiler_params=PARAMS,
            name="sum",
        )(parts)

    parts = exchange(summed(parts, far), FAR)
    total = exchange(summed(parts, near), NEAR).reshape(GRAD_ROWS, 128)
    parent, conv_total, down_total = pl.pallas_call(
        lambda *refs: final_kernel(scale, *refs),
        out_shape=(shape((64, 512), BF), shape((1728, 64), F32), shape((512, 128), F32)),
        in_specs=[SMEM] + [VMEM] * 4,
        out_specs=(VMEM,) * 3,
        compiler_params=PARAMS,
        name="final",
    )(parent_children, quads, quads1, quads2, total)
    return (parent.reshape(1, 1, 8, 8, 512), conv_total, down_total)


def solution(mesh):
    tiles, grp = mesh.devices.shape
    fine = Mesh(mesh.devices.reshape(4, tiles // 8, 2, grp), ("y", "z", "core", "grp"))
    placed = (
        P("grp", TILES, None, None, None),
        P("grp", TILES, None, None),
        P("grp", TILES, None),
        P("grp", TILES, None),
        P("grp", TILES, None),
        P("grp", TILES, None, None),
        P(),
        P(),
        P("grp", TILES, None, None, None),
    )
    return jax.shard_map(
        body,
        mesh=fine,
        in_specs=placed,
        out_specs=(P("grp", TILES, None, None, None), P(), P()),
        check_vma=False,
    )
```

```python
import math

import jax
import jax.numpy as jnp
from jax import lax
from jax.experimental import pallas as pl
from jax.experimental.pallas import tpu as pltpu
from jax.sharding import Mesh
from jax.sharding import PartitionSpec as P

BF = jnp.bfloat16
F32 = jnp.float32
TILES = ("y", "z", "z_low", "core")
NEAR = ("y", "z_low", "core", "grp")
FAR = ("z",)
DIRS = ((-1, -1), (-1, 0), (-1, 1), (0, -1), (0, 1), (1, -1), (1, 0), (1, 1))
POOL_BASE = {-1: 192, -2: 272, 1: 352, 2: 432}
DOWN_ROWS = 512
GRAD_ROWS = 1536
VMEM = pl.BlockSpec(memory_space=pltpu.VMEM)
SMEM = pl.BlockSpec(memory_space=pltpu.SMEM)
PARAMS = pltpu.CompilerParams(vmem_limit_bytes=40 * 1024 * 1024)


def iota(shape, dim):
    return lax.broadcasted_iota(jnp.int32, shape, dim)


def one_hot(hits):
    return jnp.where(hits, 1.0, 0.0).astype(BF)


def dot(a, b):
    return jnp.dot(a, b, preferred_element_type=F32)


def permuted_y(row):
    return (row & 3) * 2 + ((row >> 2) & 1)


def occ_wide(occ_ref, order):
    occ = occ_ref[...].astype(F32)
    rows = jnp.broadcast_to(occ[:, None, :], (24, 8, 64)).reshape(192, 64)
    keep = (iota((192, 64), 1) >> 3) == order(iota((192, 64), 0) & 7)
    spread = one_hot((iota((64, 512), 0) & 7) == (iota((64, 512), 1) >> 6))
    return dot(jnp.where(keep, rows, 0.0).astype(BF), spread)


def send_kernel(
    feat_hbm, occ_hbm, cot_hbm, own_ref, up_ref, down_ref, feat_ref, occ_ref, feat_sem, occ_sem, cot_sem
):
    occ_copy = pltpu.make_async_copy(occ_hbm, occ_ref, occ_sem)
    feat_copy = pltpu.make_async_copy(feat_hbm, feat_ref, feat_sem)
    cot_copy = pltpu.make_async_copy(cot_hbm, up_ref.at[0:64], cot_sem)
    occ_copy.start()
    feat_copy.start()
    cot_copy.start()
    occ_copy.wait()
    occ = occ_wide(occ_ref, lambda y: y)
    feat_copy.wait()
    own = (feat_ref[...].astype(F32) * occ).astype(BF)
    own_ref[...] = own
    row = iota((80, 192), 0)
    col = iota((80, 192), 1)
    tile = (row >= 24).astype(jnp.int32) + (row >= 48).astype(jnp.int32)
    within = row - tile * 24
    kind = within >> 3
    place = within & 7
    for ref, first, plane in ((up_ref, 64, 7), (down_ref, 0, 0)):
        src = jnp.where(
            kind == 0, plane * 8 + place, jnp.where(kind == 1, place * 8, place * 8 + 7)
        )
        src = jnp.where(row < 72, src + tile * 64, -1)
        ref[first : first + 80, :] = dot(one_hot(src == col), own).astype(BF)
    cot_copy.wait()


def merge_kernel(up_ref, down_ref, up2_ref, dn2_ref, out_ref):
    core = lax.axis_index("core")

    @pl.when(core == 0)
    def _():
        out_ref[0:144, :] = up_ref[...]
        out_ref[144:224, :] = dn2_ref[...]

    @pl.when(core != 0)
    def _():
        out_ref[0:144, :] = up2_ref[...]
        out_ref[144:224, :] = down_ref[...]


def prep_kernel(owner_ref, slot_ref, pmap_ref, occ_ref, w_ref, s_ref, sc_ref, bw_ref, occ_out, pocc_out):
    me = lax.axis_index(TILES)
    row = iota((240, 128), 0)
    lane = iota((240, 128), 1)
    off_y = (row >= 80).astype(jnp.int32) + (row >= 160).astype(jnp.int32)
    rest = row - off_y * 80
    px = rest >> 3
    py = permuted_y(rest & 7) + off_y
    sx = (px + 7) & 7
    sy = (py + 7) & 7
    side_x = (px == 9).astype(jnp.int32) - (px == 0).astype(jnp.int32)
    side_y = (py == 9).astype(jnp.int32) - (py == 0).astype(jnp.int32)
    masks = [(side_x == dx) & (side_y == dy) for dx, dy in DIRS]
    own_row = sx * 8 + sy
    for t in range(3):
        index = own_row + t * 64
        for k, (dx, dy) in enumerate(DIRS):
            owner = owner_ref[t, 0, k]
            slot = slot_ref[t, 0, k]
            off = owner - me
            here = off == 0
            base = jnp.where(
                off == -1,
                POOL_BASE[-1],
                jnp.where(off == -2, POOL_BASE[-2], jnp.where(off == 1, POOL_BASE[1], POOL_BASE[2])),
            )
            if dx:
                face, by_x, by_y = 0, 0, 1
            else:
                face, by_x, by_y = (16 if dy < 0 else 8), 1, 0
            first = jnp.where(here, slot * 64, base + slot * 24 + face)
            by_x = jnp.where(here, 8, by_x)
            by_y = jnp.where(here, 1, by_y)
            source = jnp.where(owner >= 0, first + sx * by_x + sy * by_y, -1)
            index = jnp.where(masks[k], source, index)
        for block in range(4):
            s_ref[t * 240 : (t + 1) * 240, block * 128 : (block + 1) * 128] = one_hot(
                index == lane + block * 128
            )
    row = iota((64, 256), 0)
    lane = iota((64, 256), 1)
    for t in range(3):
        owner = pmap_ref[0, 0, t]
        quad = pmap_ref[0, 1, t]
        first = (me - owner) * 64 + (quad >> 1) * 32 + (quad & 1) * 4
        index = jnp.where(owner >= 0, first + (row >> 4) * 8 + (row & 3), -1)
        sc_ref[t * 64 : (t + 1) * 64, :] = one_hot(index == lane)
    zero = jnp.zeros((64, 64), F32)
    for ab in range(9):
        w0, w1, w2 = (
            w_ref[(3 * ab + d) * 64 : (3 * ab + d + 1) * 64, :].astype(F32) for d in range(3)
        )
        bw_ref[ab * 128 : ab * 128 + 64, :] = jnp.concatenate([w2, w1, w0, zero], axis=1).astype(BF)
        bw_ref[ab * 128 + 64 : ab * 128 + 128, :] = jnp.concatenate(
            [zero, w2, w1, w0], axis=1
        ).astype(BF)
    occ = occ_wide(occ_ref, permuted_y)
    occ_out[...] = occ.astype(BF)
    wide = occ.reshape(12, 2, 8, 512)
    wide = jnp.maximum(wide[:, 0], wide[:, 1]).reshape(96, 512)
    for q in range(4):
        part = wide[:, q * 128 : (q + 1) * 128]
        part = jnp.maximum(part, pltpu.roll(part, 64, 1))
        part = part.reshape(12, 8, 128)
        part = jnp.maximum(part, pltpu.roll(part, 4, 1))
        pocc_out[:, q * 128 : (q + 1) * 128] = part.reshape(96, 128).astype(BF)


def main_kernel(
    own_ref, near_ref, up2_ref, dn2_ref, cot_ref, s_ref, sc_ref, bw_ref, occ_ref, pocc_ref,
    down_ref, quad_ref, grad_ref, xc_ref, dt_ref,
):
    pool = jnp.concatenate(
        [own_ref[...], near_ref[64:144, :], up2_ref[64:144, :], near_ref[144:224, :], dn2_ref[...]],
        axis=0,
    )
    for t in range(3):
        got = dot(s_ref[t * 240 : (t + 1) * 240, :], pool)
        for b in range(3):
            for a in range(3):
                part = got[b * 80 + a * 8 : b * 80 + a * 8 + 64].astype(BF)
                ab = 3 * a + b
                for m in range(4):
                    xc_ref[m, t * 64 : (t + 1) * 64, ab * 128 : (ab + 1) * 128] = part[
                        :, m * 128 : (m + 1) * 128
                    ]
    taps = bw_ref[...]
    outs = [dot(xc_ref[m], taps) for m in range(4)]
    shifted = []
    for j in range(5):
        total = None
        if j < 4:
            total = outs[j][:, 0:128]
        if j > 0:
            other = outs[j - 1][:, 128:256]
            total = other if total is None else total + other
        shifted.append(pltpu.roll(total, 64, 1))
    low = iota((192, 128), 1) < 64
    left = iota((192, 128), 0) & 7
    first_y = left < 4
    even_x = (iota((192, 128), 0) & 8) == 0
    down = down_ref[...]
    down_cat = jnp.concatenate([down[ij * 128 : (ij + 1) * 128] for ij in range(4)], axis=1)
    cots = jnp.concatenate(
        [cot_ref[...], near_ref[0:64, :], up2_ref[0:64, :], jnp.zeros((64, 512), BF)], axis=0
    )
    cot = dot(sc_ref[...], cots)
    pocc = pocc_ref[...].astype(F32)
    first_half = (iota((12, 8, 128), 1) & 7) < 4
    grad_down = None
    zeros = jnp.zeros((192, 128), F32)
    dt_ref[0:64, :] = jnp.zeros((64, 192), BF)
    dt_ref[576:640, :] = jnp.zeros((64, 192), BF)
    for q in range(4):
        lanes = slice(q * 128, (q + 1) * 128)
        pre = jnp.where(low, shifted[q], shifted[q + 1])
        occ = occ_ref[:, lanes].astype(F32)
        sigma = 1.0 / (1.0 + jnp.exp(-pre))
        hidden = (pre * sigma * occ).astype(BF)
        prod = dot(hidden, down_cat).reshape(12, 2, 8, 512)
        coarse = jnp.where(first_half, prod[:, 0, :, 0:128], prod[:, 0, :, 128:256]) + jnp.where(
            first_half, prod[:, 1, :, 256:384], prod[:, 1, :, 384:512]
        )
        coarse = coarse + pltpu.roll(coarse, 4, 1)
        pocc_q = pocc[:, lanes].reshape(12, 8, 128)
        coarse = (coarse * pocc_q).reshape(6, 2, 8, 128)
        coarse = jnp.where(first_half[0:6], coarse[:, 0], coarse[:, 1])
        quad_ref[:, lanes] = coarse.reshape(48, 128).astype(BF)
        pocc_rows = jnp.broadcast_to(pocc_q[:, None], (12, 2, 8, 128)).reshape(192, 128)
        gq = cot[:, lanes] * pocc_rows
        gq_bf = gq.astype(BF)
        back = lax.dot_general(gq_bf, down, (((1,), (1,)), ((), ())), preferred_element_type=F32)
        back = jnp.where(
            even_x,
            jnp.where(first_y, back[:, 0:128], back[:, 128:256]),
            jnp.where(first_y, back[:, 256:384], back[:, 384:512]),
        )
        split = jnp.concatenate(
            [
                jnp.where(even_x & first_y, gq, zeros),
                jnp.where(even_x & ~first_y, gq, zeros),
                jnp.where(~even_x & first_y, gq, zeros),
                jnp.where(~even_x & ~first_y, gq, zeros),
            ],
            axis=1,
        ).astype(BF)
        term = lax.dot_general(hidden, split, (((0,), (0,)), ((), ())), preferred_element_type=F32)
        grad_down = term if grad_down is None else grad_down + term
        delta = back * sigma * (1.0 + pre * (1.0 - sigma)) * occ
        dt_ref[64 + q * 128 : 64 + (q + 1) * 128, :] = delta.T.astype(BF)
    for ij in range(4):
        grad_ref[ij * 128 : (ij + 1) * 128, :] = grad_down[:, ij * 128 : (ij + 1) * 128].astype(BF)
    low = iota((64, 128), 1) < 64
    gconv = None
    for m in range(4):
        term = dot(dt_ref[m * 128 : m * 128 + 256, :], xc_ref[m])
        gconv = term if gconv is None else gconv + term
    held = None
    for ab in range(9):
        part = gconv[:, ab * 128 : (ab + 1) * 128]
        rows = [part[e * 64 : (e + 1) * 64] for e in range(4)]
        for d in range(3):
            value = jnp.where(low, rows[2 - d], rows[3 - d])
            value = value + pltpu.roll(value, 64, 1)
            tap = 3 * ab + d
            if tap % 2 == 0 and tap < 26:
                held = value
            else:
                pair = tap // 2
                both = jnp.where(low, held, value) if tap < 26 else jnp.where(low, value, 0.0)
                grad_ref[DOWN_ROWS + pair * 64 : DOWN_ROWS + (pair + 1) * 64, :] = both.astype(BF)
    grad_ref[DOWN_ROWS + 896 :, :] = jnp.zeros((GRAD_ROWS - DOWN_ROWS - 896, 128), BF)


def sum_kernel(parts_ref, out_ref):
    total = jnp.sum(parts_ref[...].astype(F32), axis=0).astype(BF)
    for i in range(out_ref.shape[0]):
        out_ref[i] = total


def parent_kernel(kids_ref, quad_ref, q1_ref, q2_ref, parent_ref):
    me = lax.axis_index(TILES)
    row = iota((64, 256), 0)
    lane = iota((64, 256), 1)
    which = ((row >> 5) & 1) * 2 + ((row >> 2) & 1)
    index = jnp.full((64, 256), -1, jnp.int32)
    for q in range(4):
        owner = kids_ref[0, 0, 0, q]
        first = (owner - me) * 48 + kids_ref[0, 0, 1, q] * 16
        source = jnp.where(owner >= 0, first + ((row >> 3) & 3) * 4 + (row & 3), -1)
        index = jnp.where(which == q, source, index)
    pool = jnp.concatenate(
        [quad_ref[...], q1_ref[...], q2_ref[...], jnp.zeros((112, 512), BF)], axis=0
    )
    parent_ref[...] = dot(one_hot(index == lane), pool).astype(BF)


def final_kernel(scale, grad_ref, conv_ref, down_ref):
    down_ref[...] = grad_ref[0:DOWN_ROWS, :].astype(F32) * scale
    for pair in range(14):
        block = grad_ref[DOWN_ROWS + pair * 64 : DOWN_ROWS + (pair + 1) * 64, :].astype(F32) * scale
        if pair < 13:
            conv_ref[:, pair * 128 : (pair + 1) * 128] = block
        else:
            conv_ref[:, pair * 128 : pair * 128 + 64] = block[:, 0:64]


def passed_along(shard, by):
    devices = lax.axis_size(TILES)
    pairs = [(i, i + by) for i in range(devices) if 0 <= i + by < devices]
    return lax.ppermute(shard, TILES, pairs)


def to_other_core(shard):
    return lax.ppermute(shard, "core", [(0, 1), (1, 0)])


def exchange(parts, axes):
    return lax.all_to_all(parts, axes, split_axis=0, concat_axis=0, tiled=True)


def body(
    features,
    occupancy,
    neighbour_owner,
    neighbour_slot,
    parent_map,
    parent_children,
    conv_weight,
    down_weight,
    parent_cot,
):
    shape = jax.ShapeDtypeStruct
    scale = 1.0 / math.sqrt(lax.axis_size("grp") * lax.axis_size(TILES) * 3 * 8**3)
    near, far = lax.axis_size(NEAR), lax.axis_size(FAR)
    feats = features.reshape(192, 512)
    occ = occupancy.reshape(24, 64)
    cot = parent_cot.reshape(64, 512)
    own, up, down = pl.pallas_call(
        send_kernel,
        out_shape=(shape((192, 512), BF), shape((144, 512), BF), shape((80, 512), BF)),
        in_specs=[pl.BlockSpec(memory_space=pltpu.HBM)] * 3,
        out_specs=(VMEM,) * 3,
        scratch_shapes=[pltpu.VMEM((192, 512), BF), pltpu.VMEM((24, 64), jnp.int32)]
        + [pltpu.SemaphoreType.DMA] * 3,
        compiler_params=pltpu.CompilerParams(vmem_limit_bytes=60 * 1024 * 1024),
        name="send",
    )(feats, occ, cot)
    up2, dn2 = passed_along(up, 2), passed_along(down, -2)
    pick, pick_cot, taps, occ_rows, pocc_rows = pl.pallas_call(
        prep_kernel,
        out_shape=(
            shape((720, 512), BF),
            shape((192, 256), BF),
            shape((1152, 256), BF),
            shape((192, 512), BF),
            shape((96, 512), BF),
        ),
        in_specs=[SMEM, SMEM, SMEM, VMEM, VMEM],
        out_specs=(VMEM,) * 5,
        compiler_params=PARAMS,
        cost_estimate=pl.CostEstimate(flops=10_000_000, bytes_accessed=4_000_000, transcendentals=0),
        name="prep",
    )(
        neighbour_owner.transpose(1, 0, 2),
        neighbour_slot.transpose(1, 0, 2),
        parent_map.transpose(0, 2, 1),
        occ,
        conv_weight,
    )
    up2, dn2, pick, pick_cot, taps, occ_rows, pocc_rows = lax.optimization_barrier(
        (up2, dn2, pick, pick_cot, taps, occ_rows, pocc_rows)
    )
    merged = pl.pallas_call(
        merge_kernel,
        out_shape=shape((224, 512), BF),
        in_specs=[VMEM] * 4,
        out_specs=VMEM,
        compiler_params=PARAMS,
        name="merge",
    )(up, down, up2, dn2)
    near_rows = to_other_core(merged)
    quads, grads = pl.pallas_call(
        main_kernel,
        out_shape=(shape((48, 512), BF), shape((GRAD_ROWS, 128), BF)),
        in_specs=[VMEM] * 11,
        out_specs=(VMEM,) * 2,
        scratch_shapes=[pltpu.VMEM((4, 192, 1152), BF), pltpu.VMEM((640, 192), BF)],
        compiler_params=PARAMS,
        name="main",
    )(own, near_rows, up2, dn2, cot, pick, pick_cot, taps, occ_rows, pocc_rows, down_weight)
    rows = GRAD_ROWS // near
    parts = exchange(grads.reshape(near, rows, 128), NEAR)
    quads2 = passed_along(quads, -2)
    parts, quads2 = lax.optimization_barrier((parts, quads2))

    def summed(parts, copies):
        return pl.pallas_call(
            sum_kernel,
            out_shape=shape((copies, rows, 128), BF),
            in_specs=[VMEM],
            out_specs=VMEM,
            compiler_params=PARAMS,
            name="sum",
        )(parts)

    parts = exchange(summed(parts, far), FAR)
    quads1 = to_other_core(jnp.where(lax.axis_index("core") == 0, quads2, quads))
    parent = pl.pallas_call(
        parent_kernel,
        out_shape=shape((64, 512), BF),
        in_specs=[SMEM] + [VMEM] * 3,
        out_specs=VMEM,
        compiler_params=PARAMS,
        cost_estimate=pl.CostEstimate(flops=20_000_000, bytes_accessed=300_000, transcendentals=0),
        name="parent",
    )(parent_children.transpose(0, 1, 3, 2), quads, quads1, quads2)
    parts, parent = lax.optimization_barrier((parts, parent))
    total = exchange(summed(parts, near), NEAR).reshape(GRAD_ROWS, 128)
    conv_total, down_total = pl.pallas_call(
        lambda *refs: final_kernel(scale, *refs),
        out_shape=(shape((64, 1728), F32), shape((512, 128), F32)),
        in_specs=[VMEM],
        out_specs=(VMEM,) * 2,
        compiler_params=PARAMS,
        name="final",
    )(total)
    return (parent.reshape(1, 1, 8, 8, 512), conv_total.T, down_total)


def solution(mesh):
    tiles, grp = mesh.devices.shape
    fine = Mesh(mesh.devices.reshape(4, tiles // 16, 2, 2, grp), TILES + ("grp",))
    placed = (
        P("grp", TILES, None, None, None),
        P("grp", TILES, None, None),
        P("grp", TILES, None),
        P("grp", TILES, None),
        P("grp", TILES, None),
        P("grp", TILES, None, None),
        P(),
        P(),
        P("grp", TILES, None, None, None),
    )
    return jax.shard_map(
        body,
        mesh=fine,
        in_specs=placed,
        out_specs=(P("grp", TILES, None, None, None), P(), P()),
        check_vma=False,
    )
```

```python
import math

import jax
import jax.numpy as jnp
from jax import lax
from jax.experimental import pallas as pl
from jax.experimental.pallas import tpu as pltpu
from jax.sharding import Mesh
from jax.sharding import PartitionSpec as P

BF = jnp.bfloat16
F32 = jnp.float32
TILES = ("y", "z", "z_low", "core")
NEAR = ("y", "z_low", "core", "grp")
FAR = ("z",)
DIRS = ((-1, -1), (-1, 0), (-1, 1), (0, -1), (0, 1), (1, -1), (1, 0), (1, 1))
POOL_BASE = {-1: 192, -2: 272, 1: 352, 2: 432}
DOWN_ROWS = 512
GRAD_ROWS = 1536
VMEM = pl.BlockSpec(memory_space=pltpu.VMEM)
SMEM = pl.BlockSpec(memory_space=pltpu.SMEM)
PARAMS = pltpu.CompilerParams(vmem_limit_bytes=40 * 1024 * 1024)


def iota(shape, dim):
    return lax.broadcasted_iota(jnp.int32, shape, dim)


def one_hot(hits):
    return jnp.where(hits, 1.0, 0.0).astype(BF)


def dot(a, b):
    return jnp.dot(a, b, preferred_element_type=F32)


def permuted_y(row):
    return (row & 3) * 2 + ((row >> 2) & 1)


def occ_wide(occ_ref, order):
    occ = occ_ref[...].astype(F32)
    rows = jnp.broadcast_to(occ[:, None, :], (24, 8, 64)).reshape(192, 64)
    keep = (iota((192, 64), 1) >> 3) == order(iota((192, 64), 0) & 7)
    spread = one_hot((iota((64, 512), 0) & 7) == (iota((64, 512), 1) >> 6))
    return dot(jnp.where(keep, rows, 0.0).astype(BF), spread)


def send_kernel(
    feat_hbm, occ_hbm, cot_hbm, own_ref, up_ref, down_ref, feat_ref, occ_ref, feat_sem, occ_sem, cot_sem
):
    occ_copy = pltpu.make_async_copy(occ_hbm, occ_ref, occ_sem)
    feat_copy = pltpu.make_async_copy(feat_hbm, feat_ref, feat_sem)
    cot_copy = pltpu.make_async_copy(cot_hbm, up_ref.at[0:64], cot_sem)
    occ_copy.start()
    feat_copy.start()
    cot_copy.start()
    occ_copy.wait()
    occ = occ_wide(occ_ref, lambda y: y)
    feat_copy.wait()
    own = (feat_ref[...].astype(F32) * occ).astype(BF)
    own_ref[...] = own
    row = iota((80, 192), 0)
    col = iota((80, 192), 1)
    tile = (row >= 24).astype(jnp.int32) + (row >= 48).astype(jnp.int32)
    within = row - tile * 24
    kind = within >> 3
    place = within & 7
    for ref, first, plane in ((up_ref, 64, 7), (down_ref, 0, 0)):
        src = jnp.where(
            kind == 0, plane * 8 + place, jnp.where(kind == 1, place * 8, place * 8 + 7)
        )
        src = jnp.where(row < 72, src + tile * 64, -1)
        ref[first : first + 80, :] = dot(one_hot(src == col), own).astype(BF)
    cot_copy.wait()


def merge_kernel(up_ref, down_ref, up2_ref, dn2_ref, out_ref):
    core = lax.axis_index("core")

    @pl.when(core == 0)
    def _():
        out_ref[0:144, :] = up_ref[...]
        out_ref[144:224, :] = dn2_ref[...]

    @pl.when(core != 0)
    def _():
        out_ref[0:144, :] = up2_ref[...]
        out_ref[144:224, :] = down_ref[...]


def prep_kernel(
    owner_ref, slot_ref, pmap_ref, kids_ref, occ_ref, w_ref, s_ref, sc_ref, sp_ref, bw_ref, occ_out, pocc_out
):
    me = lax.axis_index(TILES)
    row = iota((240, 128), 0)
    lane = iota((240, 128), 1)
    off_y = (row >= 80).astype(jnp.int32) + (row >= 160).astype(jnp.int32)
    rest = row - off_y * 80
    px = rest >> 3
    py = permuted_y(rest & 7) + off_y
    sx = (px + 7) & 7
    sy = (py + 7) & 7
    side_x = (px == 9).astype(jnp.int32) - (px == 0).astype(jnp.int32)
    side_y = (py == 9).astype(jnp.int32) - (py == 0).astype(jnp.int32)
    masks = [(side_x == dx) & (side_y == dy) for dx, dy in DIRS]
    own_row = sx * 8 + sy
    for t in range(3):
        index = own_row + t * 64
        for k, (dx, dy) in enumerate(DIRS):
            owner = owner_ref[t, 0, k]
            slot = slot_ref[t, 0, k]
            off = owner - me
            here = off == 0
            base = jnp.where(
                off == -1,
                POOL_BASE[-1],
                jnp.where(off == -2, POOL_BASE[-2], jnp.where(off == 1, POOL_BASE[1], POOL_BASE[2])),
            )
            if dx:
                face, by_x, by_y = 0, 0, 1
            else:
                face, by_x, by_y = (16 if dy < 0 else 8), 1, 0
            first = jnp.where(here, slot * 64, base + slot * 24 + face)
            by_x = jnp.where(here, 8, by_x)
            by_y = jnp.where(here, 1, by_y)
            source = jnp.where(owner >= 0, first + sx * by_x + sy * by_y, -1)
            index = jnp.where(masks[k], source, index)
        for block in range(4):
            s_ref[t * 240 : (t + 1) * 240, block * 128 : (block + 1) * 128] = one_hot(
                index == lane + block * 128
            )
    row = iota((64, 256), 0)
    lane = iota((64, 256), 1)
    for t in range(3):
        owner = pmap_ref[0, 0, t]
        quad = pmap_ref[0, 1, t]
        first = (me - owner) * 64 + (quad >> 1) * 32 + (quad & 1) * 4
        index = jnp.where(owner >= 0, first + (row >> 4) * 8 + (row & 3), -1)
        sc_ref[t * 64 : (t + 1) * 64, :] = one_hot(index == lane)
    which = ((row >> 5) & 1) * 2 + ((row >> 2) & 1)
    index = jnp.full((64, 256), -1, jnp.int32)
    for q in range(4):
        owner = kids_ref[0, 0, 0, q]
        first = (owner - me) * 48 + kids_ref[0, 0, 1, q] * 16
        source = jnp.where(owner >= 0, first + ((row >> 3) & 3) * 4 + (row & 3), -1)
        index = jnp.where(which == q, source, index)
    sp_ref[...] = one_hot(index == lane)
    zero = jnp.zeros((64, 64), F32)
    for ab in range(9):
        w0, w1, w2 = (
            w_ref[(3 * ab + d) * 64 : (3 * ab + d + 1) * 64, :].astype(F32) for d in range(3)
        )
        bw_ref[ab * 128 : ab * 128 + 64, :] = jnp.concatenate([w2, w1, w0, zero], axis=1).astype(BF)
        bw_ref[ab * 128 + 64 : ab * 128 + 128, :] = jnp.concatenate(
            [zero, w2, w1, w0], axis=1
        ).astype(BF)
    occ = occ_wide(occ_ref, permuted_y)
    occ_out[...] = occ.astype(BF)
    wide = occ.reshape(12, 2, 8, 512)
    wide = jnp.maximum(wide[:, 0], wide[:, 1]).reshape(96, 512)
    for q in range(4):
        part = wide[:, q * 128 : (q + 1) * 128]
        part = jnp.maximum(part, pltpu.roll(part, 64, 1))
        part = part.reshape(12, 8, 128)
        part = jnp.maximum(part, pltpu.roll(part, 4, 1))
        pocc_out[:, q * 128 : (q + 1) * 128] = part.reshape(96, 128).astype(BF)


def main_kernel(
    own_ref, near_ref, up2_ref, dn2_ref, cot_ref, s_ref, sc_ref, bw_ref, occ_ref, pocc_ref,
    down_ref, quad_ref, grad_ref, xc_ref, dt_ref,
):
    pool = jnp.concatenate(
        [own_ref[...], near_ref[64:144, :], up2_ref[64:144, :], near_ref[144:224, :], dn2_ref[...]],
        axis=0,
    )
    for t in range(3):
        got = dot(s_ref[t * 240 : (t + 1) * 240, :], pool)
        for b in range(3):
            for a in range(3):
                part = got[b * 80 + a * 8 : b * 80 + a * 8 + 64].astype(BF)
                ab = 3 * a + b
                for m in range(4):
                    xc_ref[m, t * 64 : (t + 1) * 64, ab * 128 : (ab + 1) * 128] = part[
                        :, m * 128 : (m + 1) * 128
                    ]
    taps = bw_ref[...]
    outs = [dot(xc_ref[m], taps) for m in range(4)]
    shifted = []
    for j in range(5):
        total = None
        if j < 4:
            total = outs[j][:, 0:128]
        if j > 0:
            other = outs[j - 1][:, 128:256]
            total = other if total is None else total + other
        shifted.append(pltpu.roll(total, 64, 1))
    low = iota((192, 128), 1) < 64
    left = iota((192, 128), 0) & 7
    first_y = left < 4
    even_x = (iota((192, 128), 0) & 8) == 0
    down = down_ref[...]
    down_cat = jnp.concatenate([down[ij * 128 : (ij + 1) * 128] for ij in range(4)], axis=1)
    cots = jnp.concatenate(
        [cot_ref[...], near_ref[0:64, :], up2_ref[0:64, :], jnp.zeros((64, 512), BF)], axis=0
    )
    cot = dot(sc_ref[...], cots)
    pocc = pocc_ref[...].astype(F32)
    first_half = (iota((12, 8, 128), 1) & 7) < 4
    grad_down = None
    zeros = jnp.zeros((192, 128), F32)
    dt_ref[0:64, :] = jnp.zeros((64, 192), BF)
    dt_ref[576:640, :] = jnp.zeros((64, 192), BF)
    for q in range(4):
        lanes = slice(q * 128, (q + 1) * 128)
        pre = jnp.where(low, shifted[q], shifted[q + 1])
        occ = occ_ref[:, lanes].astype(F32)
        sigma = 1.0 / (1.0 + jnp.exp(-pre))
        hidden = (pre * sigma * occ).astype(BF)
        prod = dot(hidden, down_cat).reshape(12, 2, 8, 512)
        coarse = jnp.where(first_half, prod[:, 0, :, 0:128], prod[:, 0, :, 128:256]) + jnp.where(
            first_half, prod[:, 1, :, 256:384], prod[:, 1, :, 384:512]
        )
        coarse = coarse + pltpu.roll(coarse, 4, 1)
        pocc_q = pocc[:, lanes].reshape(12, 8, 128)
        coarse = (coarse * pocc_q).reshape(6, 2, 8, 128)
        coarse = jnp.where(first_half[0:6], coarse[:, 0], coarse[:, 1])
        quad_ref[:, lanes] = coarse.reshape(48, 128).astype(BF)
        pocc_rows = jnp.broadcast_to(pocc_q[:, None], (12, 2, 8, 128)).reshape(192, 128)
        gq = cot[:, lanes] * pocc_rows
        gq_bf = gq.astype(BF)
        back = lax.dot_general(gq_bf, down, (((1,), (1,)), ((), ())), preferred_element_type=F32)
        back = jnp.where(
            even_x,
            jnp.where(first_y, back[:, 0:128], back[:, 128:256]),
            jnp.where(first_y, back[:, 256:384], back[:, 384:512]),
        )
        split = jnp.concatenate(
            [
                jnp.where(even_x & first_y, gq, zeros),
                jnp.where(even_x & ~first_y, gq, zeros),
                jnp.where(~even_x & first_y, gq, zeros),
                jnp.where(~even_x & ~first_y, gq, zeros),
            ],
            axis=1,
        ).astype(BF)
        term = lax.dot_general(hidden, split, (((0,), (0,)), ((), ())), preferred_element_type=F32)
        grad_down = term if grad_down is None else grad_down + term
        delta = back * sigma * (1.0 + pre * (1.0 - sigma)) * occ
        dt_ref[64 + q * 128 : 64 + (q + 1) * 128, :] = delta.T.astype(BF)
    for ij in range(4):
        grad_ref[ij * 128 : (ij + 1) * 128, :] = grad_down[:, ij * 128 : (ij + 1) * 128].astype(BF)
    low = iota((64, 128), 1) < 64
    gconv = None
    for m in range(4):
        term = dot(dt_ref[m * 128 : m * 128 + 256, :], xc_ref[m])
        gconv = term if gconv is None else gconv + term
    held = None
    for ab in range(9):
        part = gconv[:, ab * 128 : (ab + 1) * 128]
        rows = [part[e * 64 : (e + 1) * 64] for e in range(4)]
        for d in range(3):
            value = jnp.where(low, rows[2 - d], rows[3 - d])
            value = value + pltpu.roll(value, 64, 1)
            tap = 3 * ab + d
            if tap % 2 == 0 and tap < 26:
                held = value
            else:
                pair = tap // 2
                both = jnp.where(low, held, value) if tap < 26 else jnp.where(low, value, 0.0)
                grad_ref[DOWN_ROWS + pair * 64 : DOWN_ROWS + (pair + 1) * 64, :] = both.astype(BF)
    grad_ref[DOWN_ROWS + 896 :, :] = jnp.zeros((GRAD_ROWS - DOWN_ROWS - 896, 128), BF)


def sum_kernel(parts_ref, out_ref):
    total = jnp.sum(parts_ref[...].astype(F32), axis=0).astype(BF)
    for i in range(out_ref.shape[0]):
        out_ref[i] = total


def final_kernel(scale, sp_ref, quad_ref, q1_ref, q2_ref, grad_ref, parent_ref, conv_ref, down_ref):
    pool = jnp.concatenate(
        [quad_ref[...], q1_ref[...], q2_ref[...], jnp.zeros((112, 512), BF)], axis=0
    )
    parent_ref[...] = dot(sp_ref[...], pool).astype(BF)
    down_ref[...] = grad_ref[0:DOWN_ROWS, :].astype(F32) * scale
    for pair in range(14):
        block = grad_ref[DOWN_ROWS + pair * 64 : DOWN_ROWS + (pair + 1) * 64, :].astype(F32) * scale
        if pair < 13:
            conv_ref[:, pair * 128 : (pair + 1) * 128] = block
        else:
            conv_ref[:, pair * 128 : pair * 128 + 64] = block[:, 0:64]


def passed_along(shard, by):
    devices = lax.axis_size(TILES)
    pairs = [(i, i + by) for i in range(devices) if 0 <= i + by < devices]
    return lax.ppermute(shard, TILES, pairs)


def to_other_core(shard):
    return lax.ppermute(shard, "core", [(0, 1), (1, 0)])


def exchange(parts, axes):
    return lax.all_to_all(parts, axes, split_axis=0, concat_axis=0, tiled=True)


def body(
    features,
    occupancy,
    neighbour_owner,
    neighbour_slot,
    parent_map,
    parent_children,
    conv_weight,
    down_weight,
    parent_cot,
):
    shape = jax.ShapeDtypeStruct
    scale = 1.0 / math.sqrt(lax.axis_size("grp") * lax.axis_size(TILES) * 3 * 8**3)
    near, far = lax.axis_size(NEAR), lax.axis_size(FAR)
    feats = features.reshape(192, 512)
    occ = occupancy.reshape(24, 64)
    cot = parent_cot.reshape(64, 512)
    own, up, down = pl.pallas_call(
        send_kernel,
        out_shape=(shape((192, 512), BF), shape((144, 512), BF), shape((80, 512), BF)),
        in_specs=[pl.BlockSpec(memory_space=pltpu.HBM)] * 3,
        out_specs=(VMEM,) * 3,
        scratch_shapes=[pltpu.VMEM((192, 512), BF), pltpu.VMEM((24, 64), jnp.int32)]
        + [pltpu.SemaphoreType.DMA] * 3,
        compiler_params=pltpu.CompilerParams(vmem_limit_bytes=60 * 1024 * 1024),
        name="send",
    )(feats, occ, cot)
    up2, dn2 = passed_along(up, 2), passed_along(down, -2)
    pick, pick_cot, pick_kids, taps, occ_rows, pocc_rows = pl.pallas_call(
        prep_kernel,
        out_shape=(
            shape((720, 512), BF),
            shape((192, 256), BF),
            shape((64, 256), BF),
            shape((1152, 256), BF),
            shape((192, 512), BF),
            shape((96, 512), BF),
        ),
        in_specs=[SMEM] * 4 + [VMEM] * 2,
        out_specs=(VMEM,) * 6,
        compiler_params=PARAMS,
        cost_estimate=pl.CostEstimate(flops=10_000_000, bytes_accessed=4_000_000, transcendentals=0),
        name="prep",
    )(
        neighbour_owner.transpose(1, 0, 2),
        neighbour_slot.transpose(1, 0, 2),
        parent_map.transpose(0, 2, 1),
        parent_children.transpose(0, 1, 3, 2),
        occ,
        conv_weight,
    )
    up2, dn2, pick, pick_cot, pick_kids, taps, occ_rows, pocc_rows = lax.optimization_barrier(
        (up2, dn2, pick, pick_cot, pick_kids, taps, occ_rows, pocc_rows)
    )
    merged = pl.pallas_call(
        merge_kernel,
        out_shape=shape((224, 512), BF),
        in_specs=[VMEM] * 4,
        out_specs=VMEM,
        compiler_params=PARAMS,
        name="merge",
    )(up, down, up2, dn2)
    near_rows = to_other_core(merged)
    quads, grads = pl.pallas_call(
        main_kernel,
        out_shape=(shape((48, 512), BF), shape((GRAD_ROWS, 128), BF)),
        in_specs=[VMEM] * 11,
        out_specs=(VMEM,) * 2,
        scratch_shapes=[pltpu.VMEM((4, 192, 1152), BF), pltpu.VMEM((640, 192), BF)],
        compiler_params=PARAMS,
        name="main",
    )(own, near_rows, up2, dn2, cot, pick, pick_cot, taps, occ_rows, pocc_rows, down_weight)
    rows = GRAD_ROWS // near
    parts = exchange(grads.reshape(near, rows, 128), NEAR)
    parts, quads = lax.optimization_barrier((parts, quads))

    def summed(parts, copies):
        return pl.pallas_call(
            sum_kernel,
            out_shape=shape((copies, rows, 128), BF),
            in_specs=[VMEM],
            out_specs=VMEM,
            compiler_params=PARAMS,
            name="sum",
        )(parts)

    parts = exchange(summed(parts, far), FAR)
    quads2, quads1 = passed_along(quads, -2), passed_along(quads, -1)
    parts, quads1, quads2 = lax.optimization_barrier((parts, quads1, quads2))
    total = exchange(summed(parts, near), NEAR).reshape(GRAD_ROWS, 128)
    parent, conv_total, down_total = pl.pallas_call(
        lambda *refs: final_kernel(scale, *refs),
        out_shape=(shape((64, 512), BF), shape((64, 1728), F32), shape((512, 128), F32)),
        in_specs=[VMEM] * 5,
        out_specs=(VMEM,) * 3,
        compiler_params=PARAMS,
        name="final",
    )(pick_kids, quads, quads1, quads2, total)
    return (parent.reshape(1, 1, 8, 8, 512), conv_total.T, down_total)


def solution(mesh):
    tiles, grp = mesh.devices.shape
    fine = Mesh(mesh.devices.reshape(4, tiles // 16, 2, 2, grp), TILES + ("grp",))
    placed = (
        P("grp", TILES, None, None, None),
        P("grp", TILES, None, None),
        P("grp", TILES, None),
        P("grp", TILES, None),
        P("grp", TILES, None),
        P("grp", TILES, None, None),
        P(),
        P(),
        P("grp", TILES, None, None, None),
    )
    return jax.shard_map(
        body,
        mesh=fine,
        in_specs=placed,
        out_specs=(P("grp", TILES, None, None, None), P(), P()),
        check_vma=False,
    )
```

```python
import math

import jax
import jax.numpy as jnp
from jax import lax
from jax.experimental import pallas as pl
from jax.experimental.pallas import tpu as pltpu
from jax.sharding import Mesh
from jax.sharding import PartitionSpec as P

BF = jnp.bfloat16
F32 = jnp.float32
TILES = ("y", "z", "z_low", "core")
NEAR = ("y", "z_low", "core", "grp")
FAR = ("z",)
DIRS = ((-1, -1), (-1, 0), (-1, 1), (0, -1), (0, 1), (1, -1), (1, 0), (1, 1))
POOL_BASE = {-1: 192, -2: 272, 1: 352, 2: 432}
DOWN_ROWS = 512
GRAD_ROWS = 1536
VMEM = pl.BlockSpec(memory_space=pltpu.VMEM)
SMEM = pl.BlockSpec(memory_space=pltpu.SMEM)
PARAMS = pltpu.CompilerParams(vmem_limit_bytes=40 * 1024 * 1024)


def iota(shape, dim):
    return lax.broadcasted_iota(jnp.int32, shape, dim)


def one_hot(hits):
    return jnp.where(hits, 1.0, 0.0).astype(BF)


def dot(a, b):
    return jnp.dot(a, b, preferred_element_type=F32)


def permuted_y(row):
    return (row & 3) * 2 + ((row >> 2) & 1)


def occ_wide(occ_ref, order):
    occ = occ_ref[...].astype(F32)
    rows = jnp.broadcast_to(occ[:, None, :], (24, 8, 64)).reshape(192, 64)
    keep = (iota((192, 64), 1) >> 3) == order(iota((192, 64), 0) & 7)
    spread = one_hot((iota((64, 512), 0) & 7) == (iota((64, 512), 1) >> 6))
    return dot(jnp.where(keep, rows, 0.0).astype(BF), spread)


def send_kernel(
    feat_hbm, occ_hbm, cot_hbm, own_ref, up_ref, down_ref, feat_ref, occ_ref, feat_sem, occ_sem, cot_sem
):
    occ_copy = pltpu.make_async_copy(occ_hbm, occ_ref, occ_sem)
    feat_copy = pltpu.make_async_copy(feat_hbm, feat_ref, feat_sem)
    cot_copy = pltpu.make_async_copy(cot_hbm, up_ref.at[0:64], cot_sem)
    occ_copy.start()
    feat_copy.start()
    cot_copy.start()
    occ_copy.wait()
    occ = occ_wide(occ_ref, lambda y: y)
    feat_copy.wait()
    own = (feat_ref[...].astype(F32) * occ).astype(BF)
    own_ref[...] = own
    row = iota((80, 192), 0)
    col = iota((80, 192), 1)
    tile = (row >= 24).astype(jnp.int32) + (row >= 48).astype(jnp.int32)
    within = row - tile * 24
    kind = within >> 3
    place = within & 7
    for ref, first, plane in ((up_ref, 64, 7), (down_ref, 0, 0)):
        src = jnp.where(
            kind == 0, plane * 8 + place, jnp.where(kind == 1, place * 8, place * 8 + 7)
        )
        src = jnp.where(row < 72, src + tile * 64, -1)
        ref[first : first + 80, :] = dot(one_hot(src == col), own).astype(BF)
    cot_copy.wait()


def merge_kernel(up_ref, down_ref, up2_ref, dn2_ref, out_ref):
    core = lax.axis_index("core")

    @pl.when(core == 0)
    def _():
        out_ref[0:144, :] = up_ref[...]
        out_ref[144:224, :] = dn2_ref[...]

    @pl.when(core != 0)
    def _():
        out_ref[0:144, :] = up2_ref[...]
        out_ref[144:224, :] = down_ref[...]


def prep_kernel(
    owner_ref, slot_ref, pmap_ref, kids_ref, occ_ref, w_ref, s_ref, sc_ref, sp_ref, bw_ref, occ_out, pocc_out
):
    me = lax.axis_index(TILES)
    row = iota((240, 128), 0)
    lane = iota((240, 128), 1)
    off_y = (row >= 80).astype(jnp.int32) + (row >= 160).astype(jnp.int32)
    rest = row - off_y * 80
    px = rest >> 3
    py = permuted_y(rest & 7) + off_y
    sx = (px + 7) & 7
    sy = (py + 7) & 7
    side_x = (px == 9).astype(jnp.int32) - (px == 0).astype(jnp.int32)
    side_y = (py == 9).astype(jnp.int32) - (py == 0).astype(jnp.int32)
    masks = [(side_x == dx) & (side_y == dy) for dx, dy in DIRS]
    own_row = sx * 8 + sy
    for t in range(3):
        index = own_row + t * 64
        for k, (dx, dy) in enumerate(DIRS):
            owner = owner_ref[t, 0, k]
            slot = slot_ref[t, 0, k]
            off = owner - me
            here = off == 0
            base = jnp.where(
                off == -1,
                POOL_BASE[-1],
                jnp.where(off == -2, POOL_BASE[-2], jnp.where(off == 1, POOL_BASE[1], POOL_BASE[2])),
            )
            if dx:
                face, by_x, by_y = 0, 0, 1
            else:
                face, by_x, by_y = (16 if dy < 0 else 8), 1, 0
            first = jnp.where(here, slot * 64, base + slot * 24 + face)
            by_x = jnp.where(here, 8, by_x)
            by_y = jnp.where(here, 1, by_y)
            source = jnp.where(owner >= 0, first + sx * by_x + sy * by_y, -1)
            index = jnp.where(masks[k], source, index)
        for block in range(4):
            s_ref[t * 240 : (t + 1) * 240, block * 128 : (block + 1) * 128] = one_hot(
                index == lane + block * 128
            )
    row = iota((64, 256), 0)
    lane = iota((64, 256), 1)
    for t in range(3):
        owner = pmap_ref[0, 0, t]
        quad = pmap_ref[0, 1, t]
        first = (me - owner) * 64 + (quad >> 1) * 32 + (quad & 1) * 4
        index = jnp.where(owner >= 0, first + (row >> 4) * 8 + (row & 3), -1)
        sc_ref[t * 64 : (t + 1) * 64, :] = one_hot(index == lane)
    which = ((row >> 5) & 1) * 2 + ((row >> 2) & 1)
    index = jnp.full((64, 256), -1, jnp.int32)
    for q in range(4):
        owner = kids_ref[0, 0, 0, q]
        first = (owner - me) * 48 + kids_ref[0, 0, 1, q] * 16
        source = jnp.where(owner >= 0, first + ((row >> 3) & 3) * 4 + (row & 3), -1)
        index = jnp.where(which == q, source, index)
    sp_ref[...] = one_hot(index == lane)
    zero = jnp.zeros((64, 64), F32)
    for ab in range(9):
        w0, w1, w2 = (
            w_ref[(3 * ab + d) * 64 : (3 * ab + d + 1) * 64, :].astype(F32) for d in range(3)
        )
        bw_ref[ab * 128 : ab * 128 + 64, :] = jnp.concatenate([w2, w1, w0, zero], axis=1).astype(BF)
        bw_ref[ab * 128 + 64 : ab * 128 + 128, :] = jnp.concatenate(
            [zero, w2, w1, w0], axis=1
        ).astype(BF)
    occ = occ_wide(occ_ref, permuted_y)
    occ_out[...] = occ.astype(BF)
    wide = occ.reshape(12, 2, 8, 512)
    wide = jnp.maximum(wide[:, 0], wide[:, 1]).reshape(96, 512)
    for q in range(4):
        part = wide[:, q * 128 : (q + 1) * 128]
        part = jnp.maximum(part, pltpu.roll(part, 64, 1))
        part = part.reshape(12, 8, 128)
        part = jnp.maximum(part, pltpu.roll(part, 4, 1))
        pocc_out[:, q * 128 : (q + 1) * 128] = part.reshape(96, 128).astype(BF)


def main_kernel(
    own_ref, near_ref, up2_ref, dn2_ref, cot_ref, s_ref, sc_ref, bw_ref, occ_ref, pocc_ref,
    down_ref, quad_ref, grad_ref, xc_ref, dt_ref,
):
    pool = jnp.concatenate(
        [own_ref[...], near_ref[64:144, :], up2_ref[64:144, :], near_ref[144:224, :], dn2_ref[...]],
        axis=0,
    )
    for t in range(3):
        got = dot(s_ref[t * 240 : (t + 1) * 240, :], pool)
        for b in range(3):
            for a in range(3):
                part = got[b * 80 + a * 8 : b * 80 + a * 8 + 64].astype(BF)
                ab = 3 * a + b
                for m in range(4):
                    xc_ref[m, t * 64 : (t + 1) * 64, ab * 128 : (ab + 1) * 128] = part[
                        :, m * 128 : (m + 1) * 128
                    ]
    taps = bw_ref[...]
    outs = [dot(xc_ref[m], taps) for m in range(4)]
    shifted = []
    for j in range(5):
        total = None
        if j < 4:
            total = outs[j][:, 0:128]
        if j > 0:
            other = outs[j - 1][:, 128:256]
            total = other if total is None else total + other
        shifted.append(pltpu.roll(total, 64, 1))
    low = iota((192, 128), 1) < 64
    left = iota((192, 128), 0) & 7
    first_y = left < 4
    even_x = (iota((192, 128), 0) & 8) == 0
    down = down_ref[...]
    down_cat = jnp.concatenate([down[ij * 128 : (ij + 1) * 128] for ij in range(4)], axis=1)
    cots = jnp.concatenate(
        [cot_ref[...], near_ref[0:64, :], up2_ref[0:64, :], jnp.zeros((64, 512), BF)], axis=0
    )
    cot = dot(sc_ref[...], cots)
    pocc = pocc_ref[...].astype(F32)
    first_half = (iota((12, 8, 128), 1) & 7) < 4
    grad_down = None
    zeros = jnp.zeros((192, 128), F32)
    dt_ref[0:64, :] = jnp.zeros((64, 192), BF)
    dt_ref[576:640, :] = jnp.zeros((64, 192), BF)
    for q in range(4):
        lanes = slice(q * 128, (q + 1) * 128)
        pre = jnp.where(low, shifted[q], shifted[q + 1])
        occ = occ_ref[:, lanes].astype(F32)
        sigma = 1.0 / (1.0 + jnp.exp(-pre))
        hidden = (pre * sigma * occ).astype(BF)
        prod = dot(hidden, down_cat).reshape(12, 2, 8, 512)
        coarse = jnp.where(first_half, prod[:, 0, :, 0:128], prod[:, 0, :, 128:256]) + jnp.where(
            first_half, prod[:, 1, :, 256:384], prod[:, 1, :, 384:512]
        )
        coarse = coarse + pltpu.roll(coarse, 4, 1)
        pocc_q = pocc[:, lanes].reshape(12, 8, 128)
        coarse = (coarse * pocc_q).reshape(6, 2, 8, 128)
        coarse = jnp.where(first_half[0:6], coarse[:, 0], coarse[:, 1])
        quad_ref[:, lanes] = coarse.reshape(48, 128).astype(BF)
        pocc_rows = jnp.broadcast_to(pocc_q[:, None], (12, 2, 8, 128)).reshape(192, 128)
        gq = cot[:, lanes] * pocc_rows
        gq_bf = gq.astype(BF)
        back = lax.dot_general(gq_bf, down, (((1,), (1,)), ((), ())), preferred_element_type=F32)
        back = jnp.where(
            even_x,
            jnp.where(first_y, back[:, 0:128], back[:, 128:256]),
            jnp.where(first_y, back[:, 256:384], back[:, 384:512]),
        )
        split = jnp.concatenate(
            [
                jnp.where(even_x & first_y, gq, zeros),
                jnp.where(even_x & ~first_y, gq, zeros),
                jnp.where(~even_x & first_y, gq, zeros),
                jnp.where(~even_x & ~first_y, gq, zeros),
            ],
            axis=1,
        ).astype(BF)
        term = lax.dot_general(hidden, split, (((0,), (0,)), ((), ())), preferred_element_type=F32)
        grad_down = term if grad_down is None else grad_down + term
        delta = back * sigma * (1.0 + pre * (1.0 - sigma)) * occ
        dt_ref[64 + q * 128 : 64 + (q + 1) * 128, :] = delta.T.astype(BF)
    for ij in range(4):
        grad_ref[ij * 128 : (ij + 1) * 128, :] = grad_down[:, ij * 128 : (ij + 1) * 128].astype(BF)
    low = iota((64, 128), 1) < 64
    gconv = None
    for m in range(4):
        term = dot(dt_ref[m * 128 : m * 128 + 256, :], xc_ref[m])
        gconv = term if gconv is None else gconv + term
    held = None
    for ab in range(9):
        part = gconv[:, ab * 128 : (ab + 1) * 128]
        rows = [part[e * 64 : (e + 1) * 64] for e in range(4)]
        for d in range(3):
            value = jnp.where(low, rows[2 - d], rows[3 - d])
            value = value + pltpu.roll(value, 64, 1)
            tap = 3 * ab + d
            if tap % 2 == 0 and tap < 26:
                held = value
            else:
                pair = tap // 2
                both = jnp.where(low, held, value) if tap < 26 else jnp.where(low, value, 0.0)
                grad_ref[DOWN_ROWS + pair * 64 : DOWN_ROWS + (pair + 1) * 64, :] = both.astype(BF)
    grad_ref[DOWN_ROWS + 896 :, :] = jnp.zeros((GRAD_ROWS - DOWN_ROWS - 896, 128), BF)


def sum_kernel(rows, parts_ref, out_ref):
    parts = parts_ref[...].astype(F32)
    total = jnp.sum(parts.reshape(parts.shape[0] // rows, rows, 128), axis=0)
    copies = out_ref.shape[0] // rows
    out_ref[...] = jnp.concatenate([total] * copies, axis=0).astype(BF)


def final_kernel(scale, sp_ref, quad_ref, q1_ref, q2_ref, grad_ref, parent_ref, conv_ref, down_ref):
    pool = jnp.concatenate(
        [quad_ref[...], q1_ref[...], q2_ref[...], jnp.zeros((112, 512), BF)], axis=0
    )
    parent_ref[...] = dot(sp_ref[...], pool).astype(BF)
    down_ref[...] = grad_ref[0:DOWN_ROWS, :].astype(F32) * scale
    for pair in range(14):
        block = grad_ref[DOWN_ROWS + pair * 64 : DOWN_ROWS + (pair + 1) * 64, :].astype(F32) * scale
        if pair < 13:
            conv_ref[:, pair * 128 : (pair + 1) * 128] = block
        else:
            conv_ref[:, pair * 128 : pair * 128 + 64] = block[:, 0:64]


def passed_along(shard, by):
    devices = lax.axis_size(TILES)
    pairs = [(i, i + by) for i in range(devices) if 0 <= i + by < devices]
    return lax.ppermute(shard, TILES, pairs)


def to_other_core(shard):
    return lax.ppermute(shard, "core", [(0, 1), (1, 0)])


def exchange(parts, axes):
    return lax.all_to_all(parts, axes, split_axis=0, concat_axis=0, tiled=True)


def body(
    features,
    occupancy,
    neighbour_owner,
    neighbour_slot,
    parent_map,
    parent_children,
    conv_weight,
    down_weight,
    parent_cot,
):
    shape = jax.ShapeDtypeStruct
    scale = 1.0 / math.sqrt(lax.axis_size("grp") * lax.axis_size(TILES) * 3 * 8**3)
    near, far = lax.axis_size(NEAR), lax.axis_size(FAR)
    feats = features.reshape(192, 512)
    occ = occupancy.reshape(24, 64)
    cot = parent_cot.reshape(64, 512)
    own, up, down = pl.pallas_call(
        send_kernel,
        out_shape=(shape((192, 512), BF), shape((144, 512), BF), shape((80, 512), BF)),
        in_specs=[pl.BlockSpec(memory_space=pltpu.HBM)] * 3,
        out_specs=(VMEM,) * 3,
        scratch_shapes=[pltpu.VMEM((192, 512), BF), pltpu.VMEM((24, 64), jnp.int32)]
        + [pltpu.SemaphoreType.DMA] * 3,
        compiler_params=pltpu.CompilerParams(vmem_limit_bytes=60 * 1024 * 1024),
        name="send",
    )(feats, occ, cot)
    up2, dn2 = passed_along(up, 2), passed_along(down, -2)
    pick, pick_cot, pick_kids, taps, occ_rows, pocc_rows = pl.pallas_call(
        prep_kernel,
        out_shape=(
            shape((720, 512), BF),
            shape((192, 256), BF),
            shape((64, 256), BF),
            shape((1152, 256), BF),
            shape((192, 512), BF),
            shape((96, 512), BF),
        ),
        in_specs=[SMEM] * 4 + [VMEM] * 2,
        out_specs=(VMEM,) * 6,
        compiler_params=PARAMS,
        cost_estimate=pl.CostEstimate(flops=10_000_000, bytes_accessed=4_000_000, transcendentals=0),
        name="prep",
    )(
        neighbour_owner.transpose(1, 0, 2),
        neighbour_slot.transpose(1, 0, 2),
        parent_map.transpose(0, 2, 1),
        parent_children.transpose(0, 1, 3, 2),
        occ,
        conv_weight,
    )
    up2, dn2, pick, pick_cot, pick_kids, taps, occ_rows, pocc_rows = lax.optimization_barrier(
        (up2, dn2, pick, pick_cot, pick_kids, taps, occ_rows, pocc_rows)
    )
    merged = pl.pallas_call(
        merge_kernel,
        out_shape=shape((224, 512), BF),
        in_specs=[VMEM] * 4,
        out_specs=VMEM,
        compiler_params=PARAMS,
        name="merge",
    )(up, down, up2, dn2)
    near_rows = to_other_core(merged)
    quads, grads = pl.pallas_call(
        main_kernel,
        out_shape=(shape((48, 512), BF), shape((GRAD_ROWS, 128), BF)),
        in_specs=[VMEM] * 11,
        out_specs=(VMEM,) * 2,
        scratch_shapes=[pltpu.VMEM((4, 192, 1152), BF), pltpu.VMEM((640, 192), BF)],
        compiler_params=PARAMS,
        name="main",
    )(own, near_rows, up2, dn2, cot, pick, pick_cot, taps, occ_rows, pocc_rows, down_weight)
    rows = GRAD_ROWS // near
    parts = exchange(grads.reshape(near, rows, 128), NEAR)
    parts, quads = lax.optimization_barrier((parts, quads))

    def summed(parts, copies):
        return pl.pallas_call(
            lambda *refs: sum_kernel(rows, *refs),
            out_shape=shape((copies * rows, 128), BF),
            in_specs=[VMEM],
            out_specs=VMEM,
            compiler_params=PARAMS,
            name="sum",
        )(parts.reshape(-1, 128)).reshape(copies, rows, 128)

    parts = exchange(summed(parts, far), FAR)
    quads2, quads1 = passed_along(quads, -2), passed_along(quads, -1)
    parts, quads1, quads2 = lax.optimization_barrier((parts, quads1, quads2))
    total = exchange(summed(parts, near), NEAR).reshape(GRAD_ROWS, 128)
    parent, conv_total, down_total = pl.pallas_call(
        lambda *refs: final_kernel(scale, *refs),
        out_shape=(shape((64, 512), BF), shape((64, 1728), F32), shape((512, 128), F32)),
        in_specs=[VMEM] * 5,
        out_specs=(VMEM,) * 3,
        compiler_params=PARAMS,
        name="final",
    )(pick_kids, quads, quads1, quads2, total)
    return (parent.reshape(1, 1, 8, 8, 512), conv_total.T, down_total)


def solution(mesh):
    tiles, grp = mesh.devices.shape
    fine = Mesh(mesh.devices.reshape(4, tiles // 16, 2, 2, grp), TILES + ("grp",))
    placed = (
        P("grp", TILES, None, None, None),
        P("grp", TILES, None, None),
        P("grp", TILES, None),
        P("grp", TILES, None),
        P("grp", TILES, None),
        P("grp", TILES, None, None),
        P(),
        P(),
        P("grp", TILES, None, None, None),
    )
    return jax.shard_map(
        body,
        mesh=fine,
        in_specs=placed,
        out_specs=(P("grp", TILES, None, None, None), P(), P()),
        check_vma=False,
    )
```
